32 devices in a mesh: groups: 2 (over y), air: 4 (over z), plate: 2 (over x), field: 2 (over core).
Axes of the slice: x: 2, y: 2, z: 4, core: 2. Of those that a mesh axis runs over, the one named last changes fastest.
Arguments:
- air_prev: float32 [128, 256, 256], P(('groups', 'air'), 'plate', 'field'), parts along dimension 0, may hold values from -3 to 3
- air_now: float32 [128, 256, 256], P(('groups', 'air'), 'plate', 'field'), parts along dimension 0, may hold values from -3 to 3
- plate_prev: float32 [6, 64, 256], P('groups', 'air', 'plate'), parts along dimension 0, may hold values from -3 to 3
- plate_now: float32 [6, 64, 256], P('groups', 'air', 'plate'), parts along dimension 0, may hold values from -3 to 3
- plate_height: int32 [6], P('groups'), parts along dimension 0, may hold values from 2 to 253
- plate_rows: int32 [6, 2], P('groups'), parts along dimension 0, may hold values from 0 to 64, as said below
- plate_cols: int32 [6, 2], P('groups'), parts along dimension 0, may hold values from 0 to 256, as said below
Outputs:
- pressure_after: float32 [128, 256, 256], P(('groups', 'air'), 'plate', 'field'), parts along dimension 0
- pressure_before: float32 [128, 256, 256], P(('groups', 'air'), 'plate', 'field'), parts along dimension 0
- plate_after: float32 [6, 64, 256], P('groups', 'air', 'plate'), parts along dimension 0
- plate_before: float32 [6, 64, 256], P('groups', 'air', 'plate'), parts along dimension 0
The draws below stay inside these ranges and needn't reach their ends.
There are 2 independent parts, one for each index of `groups`. The reference program is written for one: setup_inputs(seed, part) draws one part's arguments, and reference() takes and returns one part's arrays. A program takes and returns all parts, laid end to end along the dimension named above; each array names one. Nothing has to cross between parts.
Inputs may be any that keep to these rules, and one draw needn't show every extreme that they name: `plate_rows`: row k holds a plate's first covered index and one past its last; the first lies below 16, the other at or above 48. `plate_cols`: row k holds a plate's first covered index and one past its last; the first lies below 64, the other at or above 192.
All inputs are finite; a program needn't handle non-finite values.
Results may differ from the reference program's by a relative error of at most 0.00002.
Values sent between devices are 32-bit elements; how exact they have to be, the bound alone decides.
A program may use at most 64 MiB of HBM per device.

```python
import jax
import jax.numpy as jnp
from jax import lax

PLATES = 3
NX = 64
NY = 256
NZ = 256


def span_draw(key, count, total):
    subkeys = jax.random.split(key, 4)
    starts = jax.random.randint(subkeys[0], (count,), 0, total // 4)
    finishes = jax.random.randint(subkeys[1], (count,), 3 * total // 4, total + 1)
    lowest = jax.random.randint(subkeys[2], (), 0, count)
    highest = jax.random.randint(subkeys[3], (), 0, count)
    number = jnp.arange(count)
    starts = jnp.where(number == lowest, 0, starts)
    finishes = jnp.where(number == highest, total, finishes)
    return jnp.stack([starts, finishes], axis=1).astype(jnp.int32)


def draw_plate_rows(key, part):
    return span_draw(jax.random.fold_in(key, 11), PLATES, NX)


def draw_plate_cols(key, part):
    return span_draw(jax.random.fold_in(key, 23), PLATES, NY)


def steps_of(key, shape, cuts, least, top_value):
    gain, own = 1.0, jax.random.fold_in(key, 6)
    for position, shards_of in cuts:
        heights = jnp.exp(jax.random.uniform(jax.random.fold_in(own, position), (shards_of,), jnp.float32, least / len(cuts), top_value / len(cuts)))
        gain = gain * jnp.repeat(heights, shape[position] // shards_of).reshape([-1 if axis == position else 1 for axis in range(len(shape))])
    return gain


def bell_draw(rng, shape, scale, bound, pieces=(), kind=jnp.bfloat16):
    loudness = steps_of(rng, shape, pieces, -0.22, 0.18) if pieces else 1.0
    entries = jax.random.normal(rng, shape, jnp.float32) * scale * loudness
    return jnp.minimum(jnp.maximum(entries, -bound), bound).astype(kind)


def setup_inputs(seed: int = 0, part: int = 0) -> dict:
    key_of = jax.random.split(jax.random.key(seed), 8)
    own_keys = jax.random.split(jax.random.fold_in(key_of[7], part), 8)
    return {
        "air_prev": bell_draw(own_keys[0], (NX, NY, NZ), 0.5, 3.0, ((0, 4), (1, 2), (2, 2)), jnp.float32),
        "air_now": bell_draw(own_keys[1], (NX, NY, NZ), 0.5, 3.0, ((0, 4), (1, 2), (2, 2)), jnp.float32),
        "plate_prev": bell_draw(own_keys[2], (PLATES, NX, NY), 0.5, 3.0, ((1, 4), (2, 2)), jnp.float32),
        "plate_now": bell_draw(own_keys[3], (PLATES, NX, NY), 0.5, 3.0, ((1, 4), (2, 2)), jnp.float32),
        "plate_height": jax.random.randint(own_keys[4], (PLATES,), 2, NZ - 2).astype(jnp.int32),
        "plate_rows": draw_plate_rows(jax.random.fold_in(jax.random.fold_in(key_of[7], part), 71), part),
        "plate_cols": draw_plate_cols(jax.random.fold_in(jax.random.fold_in(key_of[7], part), 71), part),
    }


near_weight = 16.0 / 12.0
far_weight = 1.0 / 12.0
centre_weight = 7.5
air_step = 0.2
plate_step = 0.05
plate_load = 0.3
air_drive = 0.1


def lap_inner(padded):
    size_row = padded.shape[0] - 4
    size_col = padded.shape[1] - 4
    size_depth = padded.shape[2] - 4

    def window(offset_row, offset_col, offset_depth):
        return padded[offset_row:offset_row + size_row, offset_col:offset_col + size_col, offset_depth:offset_depth + size_depth]

    nearest = (window(1, 2, 2) + window(3, 2, 2)) + (window(2, 1, 2) + window(2, 3, 2)) + (window(2, 2, 1) + window(2, 2, 3))
    farther = (window(0, 2, 2) + window(4, 2, 2)) + (window(2, 0, 2) + window(2, 4, 2)) + (window(2, 2, 0) + window(2, 2, 4))
    return near_weight * nearest - far_weight * farther - centre_weight * window(2, 2, 2)


def bih_inner(padded):
    size_row = padded.shape[1] - 4
    size_col = padded.shape[2] - 4

    def window(offset_row, offset_col):
        return padded[:, offset_row:offset_row + size_row, offset_col:offset_col + size_col]

    axial_terms = (window(1, 2) + window(3, 2)) + (window(2, 1) + window(2, 3))
    diagonal = (window(1, 1) + window(1, 3)) + (window(3, 1) + window(3, 3))
    distant = (window(0, 2) + window(4, 2)) + (window(2, 0) + window(2, 4))
    return 20.0 * window(2, 2) - 8.0 * axial_terms + 2.0 * diagonal + distant


def plate_mask(plate_rows, plate_cols, row_start, col_start, row_count, col_count):
    row_index = row_start + jnp.arange(row_count, dtype=jnp.int32)
    col_index = col_start + jnp.arange(col_count, dtype=jnp.int32)
    inside_rows = (row_index[None, :] >= plate_rows[:, 0:1]) & (row_index[None, :] < plate_rows[:, 1:2])
    inside_cols = (col_index[None, :] >= plate_cols[:, 0:1]) & (col_index[None, :] < plate_cols[:, 1:2])
    return (inside_rows[:, :, None] & inside_cols[:, None, :]).astype(jnp.float32)


def reference(air_prev, air_now, plate_prev, plate_now, plate_height, plate_rows, plate_cols):
    mask = plate_mask(plate_rows, plate_cols, 0, 0, NX, NY)
    plate_back = mask * plate_prev
    plate_centre = mask * plate_now
    air_back = air_prev
    air_centre = air_now
    depth_index = jnp.arange(NZ, dtype=jnp.int32)
    results = []
    for step in range(2):
        values = []
        for number in range(PLATES):
            height = plate_height[number].astype(jnp.int32)
            upper_values = lax.dynamic_index_in_dim(air_centre, height + 1, 2, keepdims=False)
            lower_values = lax.dynamic_index_in_dim(air_centre, height - 1, 2, keepdims=False)
            values.append(upper_values - lower_values)
        jump = jnp.stack(values)
        plate_padded = jnp.pad(plate_centre, ((0, 0), (2, 2), (2, 2)))
        plate_next = mask * (2.0 * plate_centre - plate_back - plate_step * bih_inner(plate_padded) - plate_load * jump)
        motion = plate_next - plate_centre
        air_next = 2.0 * air_centre - air_back + air_step * lap_inner(jnp.pad(air_centre, 2))
        source = jnp.zeros(air_centre.shape, jnp.float32)
        for number in range(PLATES):
            profile = (depth_index == plate_height[number] + 1).astype(jnp.float32) - (depth_index == plate_height[number] - 1).astype(jnp.float32)
            source = source + motion[number][:, :, None] * profile[None, None, :]
        air_next = air_next + air_drive * source
        results.append((air_next, plate_next))
        air_back, air_centre = air_centre, air_next
        plate_back, plate_centre = plate_centre, plate_next
    return results[1][0], results[0][0], results[1][1], results[0][1]
```

```python
import functools

import jax
import jax.numpy as jnp
from jax import lax
from jax.experimental import pallas as pl
from jax.experimental.pallas import tpu as pltpu
from jax.sharding import PartitionSpec as P

F32 = jnp.float32
BF16 = jnp.bfloat16
MESH = pl.DeviceIdType.MESH
plate_step = 0.05
plate_load = 0.3
PAD = 8


def split_cat(value, axis):
    high = value.astype(BF16)
    low = (value - high.astype(F32)).astype(BF16)
    if axis == 0:
        return jnp.concatenate([high.astype(F32), low.astype(F32)], axis=0).astype(BF16)
    return jnp.concatenate([high, low], axis=1)


def kernel(
    counts,
    air_prev, air_now, plate_prev, plate_now, height, rows, cols,
    out_after, out_before, out_plate_after, out_plate_before,
    p0, p1, p2, p3, mx, sel_1, sel_1_in, sel_2, sel_2_in, drive,
    u0, u1, u1l, u1r, u2, u2l, u2r, u3,
    band, pick, weights,
    local_sem, send_sem, recv_sem,
):
    n_air, n_plate = counts
    nx, ny, nz = p0.shape
    plates = u0.shape[0]
    air, plate, field = lax.axis_index("air"), lax.axis_index("plate"), lax.axis_index("field")
    has = {
        "al": air > 0, "ah": air < n_air - 1,
        "pl": plate > 0, "ph": plate < n_plate - 1,
    }
    for a in ("al", "ah"):
        for b in ("pl", "ph"):
            has[a + b] = jnp.logical_and(has[a], has[b])
    has["f"] = None
    where = {
        "al": {"air": air - 1}, "ah": {"air": air + 1},
        "pl": {"plate": plate - 1}, "ph": {"plate": plate + 1},
        "alpl": {"air": air - 1, "plate": plate - 1}, "alph": {"air": air - 1, "plate": plate + 1},
        "ahpl": {"air": air + 1, "plate": plate - 1}, "ahph": {"air": air + 1, "plate": plate + 1},
        "f": {"field": 1 - field},
    }
    swap = {"al": "ah", "ah": "al", "pl": "ph", "ph": "pl", "": "", "f": "f"}

    def opposite(side):
        return swap[side[:2]] + swap[side[2:]]

    def when(cond, fn):
        if cond is None:
            fn()
        else:
            pl.when(cond)(fn)

    made = []

    def remote(side, src, dst):
        number = len(made)
        copy = pltpu.make_async_remote_copy(
            src_ref=src, dst_ref=dst,
            send_sem=send_sem.at[number], recv_sem=recv_sem.at[number],
            device_id=where[side], device_id_type=MESH,
        )
        made.append((side, copy))
        return number

    def start(number):
        side, copy = made[number]
        when(has[side], lambda: copy.start())

    def arrive(number):
        side, copy = made[number]
        when(has[opposite(side)], lambda: copy.wait_recv())

    def sent(number):
        side, copy = made[number]
        when(has[side], lambda: copy.wait_send())

    loads = [
        pltpu.make_async_copy(air_now, p1.at[pl.ds(2, nx), pl.ds(PAD, ny)], local_sem.at[0]),
        pltpu.make_async_copy(air_prev, p0, local_sem.at[1]),
        pltpu.make_async_copy(plate_now, u1.at[:, pl.ds(8, nx)], local_sem.at[2]),
        pltpu.make_async_copy(plate_prev, u0, local_sem.at[3]),
    ]
    for copy in loads:
        copy.start()

    barrier = pltpu.get_barrier_semaphore()
    total = jnp.int32(0)
    for side, target in where.items():
        def hail(target=target):
            pl.semaphore_signal(barrier, inc=1, device_id=target, device_id_type=MESH)
        when(has[side], hail)
        total = total + (1 if has[side] is None else has[side].astype(jnp.int32))
    pl.semaphore_wait(barrier, total)

    lo8, hi8 = pl.ds(0, 8), pl.ds(nx - 8, 8)
    own = pl.ds(8, nx)

    def plate_sends(src_own, src_lo, src_hi, mid, left, right):
        return [
            remote("al", src_lo, mid.at[:, pl.ds(8 + nx, 8)]),
            remote("ah", src_hi, mid.at[:, pl.ds(0, 8)]),
            remote("pl", src_own, right.at[:, own]),
            remote("ph", src_own, left.at[:, own]),
            remote("alpl", src_lo, right.at[:, pl.ds(8 + nx, 8)]),
            remote("alph", src_lo, left.at[:, pl.ds(8 + nx, 8)]),
            remote("ahpl", src_hi, right.at[:, pl.ds(0, 8)]),
            remote("ahph", src_hi, left.at[:, pl.ds(0, 8)]),
        ]

    def layer_send(src_ref, src_index, y_at, side, slot, dst):
        return remote(
            side,
            src_ref.at[pl.ds(src_index, 1), pl.ds(y_at, ny)],
            dst.at[pl.ds(slot, 1), pl.ds(PAD, ny)],
        )

    plates_1 = plate_sends(plate_now, plate_now.at[:, lo8], plate_now.at[:, hi8], u1, u1l, u1r)
    for number in plates_1:
        start(number)
    near_1 = [
        layer_send(air_now, 0, 0, "al", nx + 2, p1),
        layer_send(air_now, nx - 1, 0, "ah", 1, p1),
    ]
    far_1 = [
        layer_send(air_now, 1, 0, "al", nx + 3, p1),
        layer_send(air_now, nx - 2, 0, "ah", 0, p1),
    ]
    cols_1 = [
        remote("pl", air_now.at[:, pl.ds(0, 8)], p1.at[pl.ds(2, nx), pl.ds(PAD + ny, 8)]),
        remote("ph", air_now.at[:, pl.ds(ny - 8, 8)], p1.at[pl.ds(2, nx), pl.ds(0, 8)]),
    ]
    for number in near_1 + cols_1 + far_1:
        start(number)

    depth_start = field * nz
    lane8 = lax.broadcasted_iota(jnp.int32, (8, nz), 1)
    row8 = lax.broadcasted_iota(jnp.int32, (8, nz), 0)
    profile = jnp.zeros((8, nz), F32)
    for k in range(plates):
        at = lane8 + (depth_start - height[k])
        step = jnp.where(at == 1, 1.0, 0.0) - jnp.where(at == -1, 1.0, 0.0)
        profile = jnp.where(row8 == k, step, profile)
    low_field = field == 0
    edge = jnp.where(low_field, nz - 2, 0) + (row8 - plates)
    is_edge = jnp.logical_and(row8 >= plates, row8 < plates + 2)
    picks = jnp.where(jnp.logical_and(is_edge, lane8 == edge), 1.0, profile)
    picks = jnp.concatenate([picks, jnp.zeros((8, nz), F32)], axis=0).astype(BF16)
    pick[...] = jnp.concatenate([picks, picks], axis=1)
    halo_lane = jnp.where(low_field, nz, -2) + (row8 - plates)
    gap = jnp.abs(lane8 - halo_lane)
    halo_weight = jnp.where(gap == 1, 16.0, jnp.where(gap == 2, -1.0, 0.0))
    wts = jnp.where(is_edge, halo_weight, 6.0 * profile)
    weights[...] = jnp.concatenate([wts, wts], axis=0).astype(BF16)
    gap = jnp.abs(
        lax.broadcasted_iota(jnp.int32, (nz, nz), 0) - lax.broadcasted_iota(jnp.int32, (nz, nz), 1)
    )
    one = jnp.where(
        gap == 0, 30.0, jnp.where(gap == 1, 16.0, jnp.where(gap == 2, -1.0, 0.0))
    ).astype(BF16)
    band[pl.ds(0, nz), :] = one
    band[pl.ds(nz, nz), :] = one
    drive[...] = jnp.zeros(drive.shape, F32)

    def clear(ref):
        def rows_low():
            ref[pl.ds(0, 2), pl.ds(PAD, ny), :] = jnp.zeros((2, ny, nz), F32)
        def rows_high():
            ref[pl.ds(nx + 2, 2), pl.ds(PAD, ny), :] = jnp.zeros((2, ny, nz), F32)
        def cols_low():
            ref[pl.ds(2, nx), pl.ds(0, 8), :] = jnp.zeros((nx, 8, nz), F32)
        def cols_high():
            ref[pl.ds(2, nx), pl.ds(PAD + ny, 8), :] = jnp.zeros((nx, 8, nz), F32)
        pl.when(jnp.logical_not(has["al"]))(rows_low)
        pl.when(jnp.logical_not(has["ah"]))(rows_high)
        pl.when(jnp.logical_not(has["pl"]))(cols_low)
        pl.when(jnp.logical_not(has["ph"]))(cols_high)

    clear(p1)
    clear(p2)

    def prepare(value, x, sel):
        pieces = split_cat(value, 1)
        mx[x] = jnp.dot(pieces, band[...], preferred_element_type=F32)
        chosen = lax.dot_general(
            pick[...], pieces, (((1,), (1,)), ((), ())), preferred_element_type=F32
        )
        sel[pl.ds(pl.multiple_of(x * 8, 8), 8), :] = chosen[:8]

    def advance(now, back, x):
        nearest = (now[x + 1, pl.ds(PAD, ny), :] + now[x + 3, pl.ds(PAD, ny), :]) + (
            now[x + 2, pl.ds(PAD - 1, ny), :] + now[x + 2, pl.ds(PAD + 1, ny), :]
        )
        farther = (now[x, pl.ds(PAD, ny), :] + now[x + 4, pl.ds(PAD, ny), :]) + (
            now[x + 2, pl.ds(PAD - 2, ny), :] + now[x + 2, pl.ds(PAD + 2, ny), :]
        )
        pushed = lax.dot_general(
            split_cat(drive[pl.ds(pl.multiple_of(x * 8, 8), 8), :], 0), weights[...],
            (((0,), (0,)), ((), ())), preferred_element_type=F32,
        )
        return ((16.0 * nearest - farther) + (mx[x] + pushed)) * (1.0 / 60.0) - back

    row_at = lax.broadcasted_iota(jnp.int32, (nx + 16, ny), 0) + (air * nx - 8)
    lane_at = lax.broadcasted_iota(jnp.int32, (nx + 16, ny), 1)
    col_at = lane_at + plate * ny

    def plate_update(mid, left, right, back_of, sel, sel_in, k):
        inside_rows = jnp.logical_and(row_at >= rows[k, 0], row_at < rows[k, 1])

        def masked(value, shift):
            c = col_at + shift
            inside = jnp.logical_and(c >= cols[k, 0], c < cols[k, 1])
            return jnp.where(jnp.logical_and(inside_rows, inside), value, 0.0)

        c = masked(mid[k], 0)
        lft = masked(left[k], -ny)
        rgt = masked(right[k], ny)
        ym1 = pltpu.roll(jnp.where(lane_at >= ny - 1, lft, c), 1, 1)
        ym2 = pltpu.roll(jnp.where(lane_at >= ny - 2, lft, c), 2, 1)
        yp1 = pltpu.roll(jnp.where(lane_at < 1, rgt, c), ny - 1, 1)
        yp2 = pltpu.roll(jnp.where(lane_at < 2, rgt, c), ny - 2, 1)
        around = ym1 + yp1
        beside = 2.0 * around - 8.0 * c
        total = nx + 16
        bih = (
            (20.0 * c - 8.0 * around + (ym2 + yp2))
            + (pltpu.roll(beside, 1, 0) + pltpu.roll(beside, total - 1, 0))
            + (pltpu.roll(c, 2, 0) + pltpu.roll(c, total - 2, 0))
        )[8 : 8 + nx]
        centre = c[8 : 8 + nx]
        mask = masked(jnp.ones((nx + 16, ny), F32), 0)[8 : 8 + nx]
        jump = sel[pl.ds(k, nx, stride=8), :] + sel_in[pl.ds(k, nx, stride=8), :]
        after = mask * (2.0 * centre - back_of(k, mask) - plate_step * bih - plate_load * jump)
        drive[pl.ds(k, nx, stride=8), :] = after - centre
        return after

    def take_edges(sel_in):
        for j in range(2):
            drive[pl.ds(plates + j, nx, stride=8), :] = sel_in[pl.ds(plates + j, nx, stride=8), :]

    loads[0].wait()

    @pl.loop(0, nx)
    def _(x):
        prepare(p1[x + 2, pl.ds(PAD, ny), :], x, sel_1)

    swap_1 = remote("f", sel_1, sel_1_in)
    start(swap_1)
    for copy in loads[1:]:
        copy.wait()
    for number in plates_1:
        arrive(number)
    arrive(swap_1)
    for k in range(plates):
        u2[k, own, :] = plate_update(
            u1, u1l, u1r, lambda k, mask: mask * u0[k], sel_1, sel_1_in, k
        )
    take_edges(sel_1_in)
    plates_2 = plate_sends(u2.at[:, own], u2.at[:, pl.ds(8, 8)], u2.at[:, pl.ds(nx, 8)], u2, u2l, u2r)
    for number in plates_2:
        start(number)
    for number in cols_1:
        arrive(number)

    def first(x):
        value = advance(p1, p0[x], x)
        p2[x + 2, pl.ds(PAD, ny), :] = value
        prepare(value, x, sel_2)

    arrive(near_1[1])
    first(1)
    far_low = layer_send(p2, 3, PAD, "al", nx + 3, p2)
    start(far_low)
    arrive(near_1[0])
    first(nx - 2)
    far_high = layer_send(p2, nx, PAD, "ah", 0, p2)
    start(far_high)

    @pl.loop(2, nx - 2)
    def _(x):
        first(x)

    arrive(far_1[1])
    first(0)
    near_low = layer_send(p2, 2, PAD, "al", nx + 2, p2)
    start(near_low)
    arrive(far_1[0])
    first(nx - 1)
    near_high = layer_send(p2, nx + 1, PAD, "ah", 1, p2)
    start(near_high)
    swap_2 = remote("f", sel_2, sel_2_in)
    start(swap_2)
    cols_2 = [
        remote("pl", p2.at[pl.ds(2, nx), pl.ds(PAD, 8)], p2.at[pl.ds(2, nx), pl.ds(PAD + ny, 8)]),
        remote("ph", p2.at[pl.ds(2, nx), pl.ds(ny, 8)], p2.at[pl.ds(2, nx), pl.ds(0, 8)]),
    ]
    for number in cols_2:
        start(number)
    stores = [
        pltpu.make_async_copy(p2.at[pl.ds(2, nx), pl.ds(PAD, ny)], out_before, local_sem.at[0]),
        pltpu.make_async_copy(u2.at[:, own], out_plate_before, local_sem.at[1]),
    ]
    for copy in stores:
        copy.start()

    for number in plates_2:
        arrive(number)
    arrive(swap_2)
    for k in range(plates):
        u3[k] = plate_update(
            u2, u2l, u2r, lambda k, mask: mask * u1[k, own, :], sel_2, sel_2_in, k
        )
    take_edges(sel_2_in)
    stores.append(pltpu.make_async_copy(u3, out_plate_after, local_sem.at[2]))
    stores[-1].start()
    for number in cols_2:
        arrive(number)

    def second(x):
        p3[x] = advance(p2, p1[x + 2, pl.ds(PAD, ny), :], x)

    @pl.loop(2, nx - 2)
    def _(x):
        second(x)

    stores.append(
        pltpu.make_async_copy(
            p3.at[pl.ds(2, nx - 4)], out_after.at[pl.ds(2, nx - 4)], local_sem.at[3]
        )
    )
    stores[-1].start()
    arrive(far_high)
    arrive(near_high)
    second(0)
    second(1)
    stores.append(pltpu.make_async_copy(p3.at[pl.ds(0, 2)], out_after.at[pl.ds(0, 2)], local_sem.at[4]))
    stores[-1].start()
    arrive(far_low)
    arrive(near_low)
    second(nx - 2)
    second(nx - 1)
    stores.append(
        pltpu.make_async_copy(
            p3.at[pl.ds(nx - 2, 2)], out_after.at[pl.ds(nx - 2, 2)], local_sem.at[5]
        )
    )
    stores[-1].start()
    for number in range(len(made)):
        sent(number)
    for copy in stores:
        copy.wait()


REMOTES = 30


def on_device(counts, *arrays):
    air_prev, _, plate_prev, _, _, _, _ = arrays
    nx, ny, nz = air_prev.shape
    plates = plate_prev.shape[0]
    padded = pltpu.VMEM((nx + 4, ny + 2 * PAD, nz), F32)
    block = pltpu.VMEM((nx, ny, nz), F32)
    flat = pltpu.VMEM((nx * 8, ny), F32)
    tall = pltpu.VMEM((plates, nx + 16, ny), F32)
    tile = pltpu.VMEM((plates, nx, ny), F32)
    anywhere = pl.BlockSpec(memory_space=pl.ANY)
    scalars = pl.BlockSpec(memory_space=pltpu.SMEM)
    air = jax.ShapeDtypeStruct(air_prev.shape, F32)
    plate = jax.ShapeDtypeStruct(plate_prev.shape, F32)
    return pl.pallas_call(
        functools.partial(kernel, counts),
        out_shape=(air, air, plate, plate),
        in_specs=[anywhere] * 4 + [scalars] * 3,
        out_specs=(anywhere,) * 4,
        scratch_shapes=[
            block, padded, padded, block, block, flat, flat, flat, flat, flat,
            tile, tall, tall, tall, tall, tall, tall, tile,
            pltpu.VMEM((2 * nz, nz), BF16),
            pltpu.VMEM((16, 2 * nz), BF16),
            pltpu.VMEM((16, nz), BF16),
            pltpu.SemaphoreType.DMA((6,)),
            pltpu.SemaphoreType.DMA((REMOTES,)),
            pltpu.SemaphoreType.DMA((REMOTES,)),
        ],
        compiler_params=pltpu.CompilerParams(
            collective_id=0, has_side_effects=True, vmem_limit_bytes=24 * 1024 * 1024
        ),
        cost_estimate=pl.CostEstimate(
            flops=50 * nx * ny * nz, bytes_accessed=16 * nx * ny * nz, transcendentals=0
        ),
    )(*arrays)


def solution(mesh):
    counts = (mesh.shape["air"], mesh.shape["plate"])
    air = P(("groups", "air"), "plate", "field")
    plate = P("groups", "air", "plate")
    return jax.shard_map(
        functools.partial(on_device, counts),
        mesh=mesh,
        in_specs=(air, air, plate, plate, P("groups"), P("groups", None), P("groups", None)),
        out_specs=(air, air, plate, plate),
        check_vma=False,
    )
```

```python
import functools

import jax
import jax.numpy as jnp
from jax import lax
from jax.experimental import pallas as pl
from jax.experimental.pallas import tpu as pltpu
from jax.sharding import PartitionSpec as P

F32 = jnp.float32
BF16 = jnp.bfloat16
MESH = pl.DeviceIdType.MESH
plate_step = 0.05
plate_load = 0.3
PAD = 8


def split_cat(value, axis):
    high = value.astype(BF16)
    low = (value - high.astype(F32)).astype(BF16)
    if axis == 0:
        return jnp.concatenate([high.astype(F32), low.astype(F32)], axis=0).astype(BF16)
    return jnp.concatenate([high, low], axis=1)


def kernel(
    counts,
    air_prev, air_now, plate_prev, plate_now, height_in, rows_in, cols_in,
    out_after, out_before, out_plate_after, out_plate_before,
    p0, p1, p2, mx, sel_1, sel_1_in, sel_2, sel_2_in, drive,
    u0, u1, u1l, u1r, u2, u2l, u2r,
    band, pick, weights, height, rows, cols,
    local_sem, send_sem, recv_sem,
):
    n_air, n_plate = counts
    nx, ny, nz = p0.shape
    plates = u0.shape[0]
    air, plate, field = lax.axis_index("air"), lax.axis_index("plate"), lax.axis_index("field")
    has = {
        "al": air > 0, "ah": air < n_air - 1,
        "pl": plate > 0, "ph": plate < n_plate - 1,
    }
    for a in ("al", "ah"):
        for b in ("pl", "ph"):
            has[a + b] = jnp.logical_and(has[a], has[b])
    has["f"] = None
    where = {
        "al": {"air": air - 1}, "ah": {"air": air + 1},
        "pl": {"plate": plate - 1}, "ph": {"plate": plate + 1},
        "alpl": {"air": air - 1, "plate": plate - 1}, "alph": {"air": air - 1, "plate": plate + 1},
        "ahpl": {"air": air + 1, "plate": plate - 1}, "ahph": {"air": air + 1, "plate": plate + 1},
        "f": {"field": 1 - field},
    }
    swap = {"al": "ah", "ah": "al", "pl": "ph", "ph": "pl", "": "", "f": "f"}

    def opposite(side):
        return swap[side[:2]] + swap[side[2:]]

    def when(cond, fn):
        if cond is None:
            fn()
        else:
            pl.when(cond)(fn)

    made = []

    def remote(side, src, dst):
        number = len(made)
        copy = pltpu.make_async_remote_copy(
            src_ref=src, dst_ref=dst,
            send_sem=send_sem.at[number], recv_sem=recv_sem.at[number],
            device_id=where[side], device_id_type=MESH,
        )
        made.append((side, copy))
        return number

    def start(number):
        side, copy = made[number]
        when(has[side], lambda: copy.start())

    def arrive(number):
        side, copy = made[number]
        when(has[opposite(side)], lambda: copy.wait_recv())

    def sent(number):
        side, copy = made[number]
        when(has[side], lambda: copy.wait_send())

    loads = [
        pltpu.make_async_copy(air_now, p1.at[pl.ds(2, nx), pl.ds(PAD, ny)], local_sem.at[0]),
        pltpu.make_async_copy(air_prev, p0, local_sem.at[1]),
        pltpu.make_async_copy(plate_now, u1.at[:, pl.ds(8, nx)], local_sem.at[2]),
        pltpu.make_async_copy(plate_prev, u0, local_sem.at[3]),
        pltpu.make_async_copy(height_in, height, local_sem.at[4]),
        pltpu.make_async_copy(rows_in, rows, local_sem.at[5]),
        pltpu.make_async_copy(cols_in, cols, local_sem.at[6]),
    ]
    for copy in loads:
        copy.start()

    barrier = pltpu.get_barrier_semaphore()
    total = jnp.int32(0)
    for side, target in where.items():
        def hail(target=target):
            pl.semaphore_signal(barrier, inc=1, device_id=target, device_id_type=MESH)
        when(has[side], hail)
        total = total + (1 if has[side] is None else has[side].astype(jnp.int32))
    pl.semaphore_wait(barrier, total)

    lo8, hi8 = pl.ds(0, 8), pl.ds(nx - 8, 8)
    own = pl.ds(8, nx)

    def plate_sends(src_own, src_lo, src_hi, mid, left, right):
        return [
            remote("al", src_lo, mid.at[:, pl.ds(8 + nx, 8)]),
            remote("ah", src_hi, mid.at[:, pl.ds(0, 8)]),
            remote("pl", src_own, right.at[:, own]),
            remote("ph", src_own, left.at[:, own]),
            remote("alpl", src_lo, right.at[:, pl.ds(8 + nx, 8)]),
            remote("alph", src_lo, left.at[:, pl.ds(8 + nx, 8)]),
            remote("ahpl", src_hi, right.at[:, pl.ds(0, 8)]),
            remote("ahph", src_hi, left.at[:, pl.ds(0, 8)]),
        ]

    def layer_send(src_ref, src_index, y_at, side, slot, dst):
        return remote(
            side,
            src_ref.at[pl.ds(src_index, 1), pl.ds(y_at, ny)],
            dst.at[pl.ds(slot, 1), pl.ds(PAD, ny)],
        )

    plates_1 = plate_sends(plate_now, plate_now.at[:, lo8], plate_now.at[:, hi8], u1, u1l, u1r)
    for number in plates_1:
        start(number)
    near_1 = [
        layer_send(air_now, 0, 0, "al", nx + 2, p1),
        layer_send(air_now, nx - 1, 0, "ah", 1, p1),
    ]
    far_1 = [
        layer_send(air_now, 1, 0, "al", nx + 3, p1),
        layer_send(air_now, nx - 2, 0, "ah", 0, p1),
    ]
    cols_1 = [
        remote("pl", air_now.at[:, pl.ds(0, 8)], p1.at[pl.ds(2, nx), pl.ds(PAD + ny, 8)]),
        remote("ph", air_now.at[:, pl.ds(ny - 8, 8)], p1.at[pl.ds(2, nx), pl.ds(0, 8)]),
    ]
    for number in near_1 + cols_1 + far_1:
        start(number)

    for copy in loads[4:]:
        copy.wait()
    depth_start = field * nz
    lane8 = lax.broadcasted_iota(jnp.int32, (8, nz), 1)
    row8 = lax.broadcasted_iota(jnp.int32, (8, nz), 0)
    profile = jnp.zeros((8, nz), F32)
    for k in range(plates):
        at = lane8 + (depth_start - height[k])
        step = jnp.where(at == 1, 1.0, 0.0) - jnp.where(at == -1, 1.0, 0.0)
        profile = jnp.where(row8 == k, step, profile)
    low_field = field == 0
    edge = jnp.where(low_field, nz - 2, 0) + (row8 - plates)
    is_edge = jnp.logical_and(row8 >= plates, row8 < plates + 2)
    picks = jnp.where(jnp.logical_and(is_edge, lane8 == edge), 1.0, profile)
    picks = jnp.concatenate([picks, jnp.zeros((8, nz), F32)], axis=0).astype(BF16)
    pick[...] = jnp.concatenate([picks, picks], axis=1)
    halo_lane = jnp.where(low_field, nz, -2) + (row8 - plates)
    gap = jnp.abs(lane8 - halo_lane)
    halo_weight = jnp.where(gap == 1, 16.0, jnp.where(gap == 2, -1.0, 0.0))
    wts = jnp.where(is_edge, halo_weight, 6.0 * profile)
    weights[...] = jnp.concatenate([wts, wts], axis=0).astype(BF16)
    gap = jnp.abs(
        lax.broadcasted_iota(jnp.int32, (nz, nz), 0) - lax.broadcasted_iota(jnp.int32, (nz, nz), 1)
    )
    one = jnp.where(
        gap == 0, 30.0, jnp.where(gap == 1, 16.0, jnp.where(gap == 2, -1.0, 0.0))
    ).astype(BF16)
    band[pl.ds(0, nz), :] = one
    band[pl.ds(nz, nz), :] = one
    drive[...] = jnp.zeros(drive.shape, F32)

    def clear(ref):
        def rows_low():
            ref[pl.ds(0, 2), pl.ds(PAD, ny), :] = jnp.zeros((2, ny, nz), F32)
        def rows_high():
            ref[pl.ds(nx + 2, 2), pl.ds(PAD, ny), :] = jnp.zeros((2, ny, nz), F32)
        def cols_low():
            ref[pl.ds(2, nx), pl.ds(0, 8), :] = jnp.zeros((nx, 8, nz), F32)
        def cols_high():
            ref[pl.ds(2, nx), pl.ds(PAD + ny, 8), :] = jnp.zeros((nx, 8, nz), F32)
        pl.when(jnp.logical_not(has["al"]))(rows_low)
        pl.when(jnp.logical_not(has["ah"]))(rows_high)
        pl.when(jnp.logical_not(has["pl"]))(cols_low)
        pl.when(jnp.logical_not(has["ph"]))(cols_high)

    clear(p1)
    clear(p2)

    def prepare(value, x, sel):
        pieces = split_cat(value, 1)
        mx[x] = jnp.dot(pieces, band[...], preferred_element_type=F32)
        chosen = lax.dot_general(
            pick[...], pieces, (((1,), (1,)), ((), ())), preferred_element_type=F32
        )
        sel[pl.ds(x * 8, 8), :] = chosen[:8]

    def advance(now, back, x):
        nearest = (now[x + 1, pl.ds(PAD, ny), :] + now[x + 3, pl.ds(PAD, ny), :]) + (
            now[x + 2, pl.ds(PAD - 1, ny), :] + now[x + 2, pl.ds(PAD + 1, ny), :]
        )
        farther = (now[x, pl.ds(PAD, ny), :] + now[x + 4, pl.ds(PAD, ny), :]) + (
            now[x + 2, pl.ds(PAD - 2, ny), :] + now[x + 2, pl.ds(PAD + 2, ny), :]
        )
        pushed = lax.dot_general(
            split_cat(drive[pl.ds(x * 8, 8), :], 0), weights[...],
            (((0,), (0,)), ((), ())), preferred_element_type=F32,
        )
        return ((16.0 * nearest - farther) + (mx[x] + pushed)) * (1.0 / 60.0) - back

    row_at = lax.broadcasted_iota(jnp.int32, (nx + 16, ny), 0) + (air * nx - 8)
    lane_at = lax.broadcasted_iota(jnp.int32, (nx + 16, ny), 1)
    col_at = lane_at + plate * ny

    def plate_update(mid, left, right, back_of, sel, sel_in, k):
        inside_rows = jnp.logical_and(row_at >= rows[0, k], row_at < rows[1, k])

        def masked(value, shift):
            c = col_at + shift
            inside = jnp.logical_and(c >= cols[0, k], c < cols[1, k])
            return jnp.where(jnp.logical_and(inside_rows, inside), value, 0.0)

        c = masked(mid[k], 0)
        lft = masked(left[k], -ny)
        rgt = masked(right[k], ny)
        ym1 = pltpu.roll(jnp.where(lane_at >= ny - 1, lft, c), 1, 1)
        ym2 = pltpu.roll(jnp.where(lane_at >= ny - 2, lft, c), 2, 1)
        yp1 = pltpu.roll(jnp.where(lane_at < 1, rgt, c), ny - 1, 1)
        yp2 = pltpu.roll(jnp.where(lane_at < 2, rgt, c), ny - 2, 1)
        around = ym1 + yp1
        beside = 2.0 * around - 8.0 * c
        total = nx + 16
        bih = (
            (20.0 * c - 8.0 * around + (ym2 + yp2))
            + (pltpu.roll(beside, 1, 0) + pltpu.roll(beside, total - 1, 0))
            + (pltpu.roll(c, 2, 0) + pltpu.roll(c, total - 2, 0))
        )[8 : 8 + nx]
        centre = c[8 : 8 + nx]
        mask = masked(jnp.ones((nx + 16, ny), F32), 0)[8 : 8 + nx]
        jump = sel[pl.ds(k, nx, stride=8), :] + sel_in[pl.ds(k, nx, stride=8), :]
        after = mask * (2.0 * centre - back_of(k, mask) - plate_step * bih - plate_load * jump)
        drive[pl.ds(k, nx, stride=8), :] = after - centre
        return after

    def take_edges(sel_in):
        for j in range(2):
            drive[pl.ds(plates + j, nx, stride=8), :] = sel_in[pl.ds(plates + j, nx, stride=8), :]

    loads[0].wait()

    for x in range(nx):
        prepare(p1[x + 2, pl.ds(PAD, ny), :], x, sel_1)

    swap_1 = remote("f", sel_1, sel_1_in)
    start(swap_1)
    for copy in loads[1:4]:
        copy.wait()
    for number in plates_1:
        arrive(number)
    arrive(swap_1)
    for k in range(plates):
        u2[k, own, :] = plate_update(
            u1, u1l, u1r, lambda k, mask: mask * u0[k], sel_1, sel_1_in, k
        )
    take_edges(sel_1_in)
    plates_2 = plate_sends(u2.at[:, own], u2.at[:, pl.ds(8, 8)], u2.at[:, pl.ds(nx, 8)], u2, u2l, u2r)
    for number in plates_2:
        start(number)
    for number in cols_1:
        arrive(number)

    def first(x):
        value = advance(p1, p0[x], x)
        p2[x + 2, pl.ds(PAD, ny), :] = value
        prepare(value, x, sel_2)

    arrive(near_1[1])
    first(1)
    far_low = layer_send(p2, 3, PAD, "al", nx + 3, p2)
    start(far_low)
    arrive(near_1[0])
    first(nx - 2)
    far_high = layer_send(p2, nx, PAD, "ah", 0, p2)
    start(far_high)

    for x in range(2, nx - 2):
        first(x)

    arrive(far_1[1])
    first(0)
    near_low = layer_send(p2, 2, PAD, "al", nx + 2, p2)
    start(near_low)
    arrive(far_1[0])
    first(nx - 1)
    near_high = layer_send(p2, nx + 1, PAD, "ah", 1, p2)
    start(near_high)
    swap_2 = remote("f", sel_2, sel_2_in)
    start(swap_2)
    cols_2 = [
        remote("pl", p2.at[pl.ds(2, nx), pl.ds(PAD, 8)], p2.at[pl.ds(2, nx), pl.ds(PAD + ny, 8)]),
        remote("ph", p2.at[pl.ds(2, nx), pl.ds(ny, 8)], p2.at[pl.ds(2, nx), pl.ds(0, 8)]),
    ]
    for number in cols_2:
        start(number)
    stores = [
        pltpu.make_async_copy(p2.at[pl.ds(2, nx), pl.ds(PAD, ny)], out_before, local_sem.at[0]),
        pltpu.make_async_copy(u2.at[:, own], out_plate_before, local_sem.at[1]),
    ]
    for copy in stores:
        copy.start()

    for number in plates_2:
        arrive(number)
    arrive(swap_2)
    for k in range(plates):
        out_plate_after[k] = plate_update(
            u2, u2l, u2r, lambda k, mask: mask * u1[k, own, :], sel_2, sel_2_in, k
        )
    take_edges(sel_2_in)
    for number in cols_2:
        arrive(number)

    def second(x):
        out_after[x] = advance(p2, p1[x + 2, pl.ds(PAD, ny), :], x)

    for x in range(2, nx - 2):
        second(x)

    arrive(far_high)
    arrive(near_high)
    second(0)
    second(1)
    arrive(far_low)
    arrive(near_low)
    second(nx - 2)
    second(nx - 1)
    for number in range(len(made)):
        sent(number)
    for copy in stores:
        copy.wait()


REMOTES = 30


def put_kernel(*refs):
    count = (len(refs) - 1) // 2
    copies = [
        pltpu.make_async_copy(refs[i], refs[count + i], refs[-1].at[i]) for i in range(count)
    ]
    for copy in copies:
        copy.start()
    for copy in copies:
        copy.wait()


def on_device(counts, *arrays):
    air_prev, _, plate_prev, _, _, _, _ = arrays
    nx, ny, nz = air_prev.shape
    plates = plate_prev.shape[0]
    padded = pltpu.VMEM((nx + 4, ny + 2 * PAD, nz), F32)
    block = pltpu.VMEM((nx, ny, nz), F32)
    flat = pltpu.VMEM((nx * 8, ny), F32)
    tall = pltpu.VMEM((plates, nx + 16, ny), F32)
    tile = pltpu.VMEM((plates, nx, ny), F32)
    anywhere = pl.BlockSpec(memory_space=pl.ANY)
    stored = pl.BlockSpec(memory_space=pltpu.HBM)
    air = jax.ShapeDtypeStruct(air_prev.shape, F32)
    plate = jax.ShapeDtypeStruct(plate_prev.shape, F32)
    held_air = pltpu.VMEM(air.shape, F32)
    held_plate = pltpu.VMEM(plate.shape, F32)
    results = pl.pallas_call(
        functools.partial(kernel, counts),
        out_shape=(held_air, held_air, held_plate, held_plate),
        in_specs=[stored] * 7,
        out_specs=(pl.BlockSpec(memory_space=pltpu.VMEM),) * 4,
        scratch_shapes=[
            block, padded, padded, block, flat, flat, flat, flat, flat,
            tile, tall, tall, tall, tall, tall, tall,
            pltpu.VMEM((2 * nz, nz), BF16),
            pltpu.VMEM((16, 2 * nz), BF16),
            pltpu.VMEM((16, nz), BF16),
            pltpu.SMEM((plates,), jnp.int32),
            pltpu.SMEM((2, plates), jnp.int32),
            pltpu.SMEM((2, plates), jnp.int32),
            pltpu.SemaphoreType.DMA((7,)),
            pltpu.SemaphoreType.DMA((REMOTES,)),
            pltpu.SemaphoreType.DMA((REMOTES,)),
        ],
        compiler_params=pltpu.CompilerParams(
            collective_id=0, has_side_effects=True, vmem_limit_bytes=60 * 1024 * 1024
        ),
        cost_estimate=pl.CostEstimate(
            flops=50 * nx * ny * nz, bytes_accessed=16 * nx * ny * nz, transcendentals=0
        ),
    )(*arrays[:5], arrays[5].T, arrays[6].T)
    return pl.pallas_call(
        put_kernel,
        out_shape=(air, air, plate, plate),
        in_specs=[pl.BlockSpec(memory_space=pltpu.VMEM)] * 4,
        out_specs=(stored,) * 4,
        scratch_shapes=[pltpu.SemaphoreType.DMA((4,))],
        cost_estimate=pl.CostEstimate(
            flops=0, bytes_accessed=16 * nx * ny * nz, transcendentals=0
        ),
    )(*[pltpu.with_memory_space_constraint(one, pltpu.VMEM) for one in results])


def solution(mesh):
    counts = (mesh.shape["air"], mesh.shape["plate"])
    air = P(("groups", "air"), "plate", "field")
    plate = P("groups", "air", "plate")
    return jax.shard_map(
        functools.partial(on_device, counts),
        mesh=mesh,
        in_specs=(air, air, plate, plate, P("groups"), P("groups", None), P("groups", None)),
        out_specs=(air, air, plate, plate),
        check_vma=False,
    )
```

```python
import functools

import jax
import jax.numpy as jnp
from jax import lax
from jax.experimental import pallas as pl
from jax.experimental.pallas import tpu as pltpu
from jax.sharding import PartitionSpec as P

F32 = jnp.float32
BF16 = jnp.bfloat16
MESH = pl.DeviceIdType.MESH
plate_step = 0.05
plate_load = 0.3
PAD = 8


def split_cat(value, axis):
    high = value.astype(BF16)
    low = (value - high.astype(F32)).astype(BF16)
    if axis == 0:
        return jnp.concatenate([high.astype(F32), low.astype(F32)], axis=0).astype(BF16)
    return jnp.concatenate([high, low], axis=1)


def kernel(
    counts,
    air_prev, air_now, plate_prev, plate_now, height_in, rows_in, cols_in,
    out_after, out_before, out_plate_after, out_plate_before,
    p0, p1, p2, mx, sel_1, sel_1_in, sel_2, sel_2_in, drive,
    u0, u1, u1l, u1r, u2, u2l, u2r,
    band, pick, weights, height, rows, cols,
    local_sem, send_sem, recv_sem,
):
    n_air, n_plate = counts
    nx, ny, nz = p0.shape
    plates = u0.shape[0]
    air, plate, field = lax.axis_index("air"), lax.axis_index("plate"), lax.axis_index("field")
    has = {
        "al": air > 0, "ah": air < n_air - 1,
        "pl": plate > 0, "ph": plate < n_plate - 1,
    }
    for a in ("al", "ah"):
        for b in ("pl", "ph"):
            has[a + b] = jnp.logical_and(has[a], has[b])
    has["f"] = None
    where = {
        "al": {"air": air - 1}, "ah": {"air": air + 1},
        "pl": {"plate": plate - 1}, "ph": {"plate": plate + 1},
        "alpl": {"air": air - 1, "plate": plate - 1}, "alph": {"air": air - 1, "plate": plate + 1},
        "ahpl": {"air": air + 1, "plate": plate - 1}, "ahph": {"air": air + 1, "plate": plate + 1},
        "f": {"field": 1 - field},
    }
    swap = {"al": "ah", "ah": "al", "pl": "ph", "ph": "pl", "": "", "f": "f"}

    def opposite(side):
        return swap[side[:2]] + swap[side[2:]]

    def when(cond, fn):
        if cond is None:
            fn()
        else:
            pl.when(cond)(fn)

    made = []

    def remote(side, src, dst):
        number = len(made)
        copy = pltpu.make_async_remote_copy(
            src_ref=src, dst_ref=dst,
            send_sem=send_sem.at[number], recv_sem=recv_sem.at[number],
            device_id=where[side], device_id_type=MESH,
        )
        made.append((side, copy))
        return number

    def start(number):
        side, copy = made[number]
        when(has[side], lambda: copy.start())

    def arrive(number):
        side, copy = made[number]
        when(has[opposite(side)], lambda: copy.wait_recv())

    def sent(number):
        side, copy = made[number]
        when(has[side], lambda: copy.wait_send())

    loads = [
        pltpu.make_async_copy(air_now, p1.at[pl.ds(2, nx), pl.ds(PAD, ny)], local_sem.at[0]),
        pltpu.make_async_copy(air_prev, p0, local_sem.at[1]),
        pltpu.make_async_copy(plate_now, u1.at[:, pl.ds(8, nx)], local_sem.at[2]),
        pltpu.make_async_copy(plate_prev, u0, local_sem.at[3]),
        pltpu.make_async_copy(height_in, height, local_sem.at[4]),
        pltpu.make_async_copy(rows_in, rows, local_sem.at[5]),
        pltpu.make_async_copy(cols_in, cols, local_sem.at[6]),
    ]
    for copy in loads:
        copy.start()

    barrier = pltpu.get_barrier_semaphore()
    total = jnp.int32(0)
    for side, target in where.items():
        def hail(target=target):
            pl.semaphore_signal(barrier, inc=1, device_id=target, device_id_type=MESH)
        when(has[side], hail)
        total = total + (1 if has[side] is None else has[side].astype(jnp.int32))
    for copy in loads[4:]:
        copy.wait()
    depth_start = field * nz
    lane8 = lax.broadcasted_iota(jnp.int32, (8, nz), 1)
    row8 = lax.broadcasted_iota(jnp.int32, (8, nz), 0)
    profile = jnp.zeros((8, nz), F32)
    for k in range(plates):
        at = lane8 + (depth_start - height[k])
        step = jnp.where(at == 1, 1.0, 0.0) - jnp.where(at == -1, 1.0, 0.0)
        profile = jnp.where(row8 == k, step, profile)
    low_field = field == 0
    edge = jnp.where(low_field, nz - 2, 0) + (row8 - plates)
    is_edge = jnp.logical_and(row8 >= plates, row8 < plates + 2)
    picks = jnp.where(jnp.logical_and(is_edge, lane8 == edge), 1.0, profile)
    picks = jnp.concatenate([picks, jnp.zeros((8, nz), F32)], axis=0).astype(BF16)
    pick[...] = jnp.concatenate([picks, picks], axis=1)
    halo_lane = jnp.where(low_field, nz, -2) + (row8 - plates)
    gap = jnp.abs(lane8 - halo_lane)
    halo_weight = jnp.where(gap == 1, 16.0, jnp.where(gap == 2, -1.0, 0.0))
    wts = jnp.where(is_edge, halo_weight, 6.0 * profile)
    weights[...] = jnp.concatenate([wts, wts], axis=0).astype(BF16)
    gap = jnp.abs(
        lax.broadcasted_iota(jnp.int32, (nz, nz), 0) - lax.broadcasted_iota(jnp.int32, (nz, nz), 1)
    )
    one = jnp.where(
        gap == 0, 30.0, jnp.where(gap == 1, 16.0, jnp.where(gap == 2, -1.0, 0.0))
    ).astype(BF16)
    band[pl.ds(0, nz), :] = one
    band[pl.ds(nz, nz), :] = one
    drive[...] = jnp.zeros(drive.shape, F32)

    def clear(ref):
        def rows_low():
            ref[pl.ds(0, 2), pl.ds(PAD, ny), :] = jnp.zeros((2, ny, nz), F32)
        def rows_high():
            ref[pl.ds(nx + 2, 2), pl.ds(PAD, ny), :] = jnp.zeros((2, ny, nz), F32)
        def cols_low():
            ref[pl.ds(2, nx), pl.ds(0, 8), :] = jnp.zeros((nx, 8, nz), F32)
        def cols_high():
            ref[pl.ds(2, nx), pl.ds(PAD + ny, 8), :] = jnp.zeros((nx, 8, nz), F32)
        pl.when(jnp.logical_not(has["al"]))(rows_low)
        pl.when(jnp.logical_not(has["ah"]))(rows_high)
        pl.when(jnp.logical_not(has["pl"]))(cols_low)
        pl.when(jnp.logical_not(has["ph"]))(cols_high)

    clear(p1)
    clear(p2)

    for copy in (loads[0], loads[2]):
        copy.wait()
    pl.semaphore_wait(barrier, total)

    own = pl.ds(8, nx)

    def plate_sends(src_own, src_lo, src_hi, mid, left, right):
        return [
            remote("al", src_lo, mid.at[:, pl.ds(8 + nx, 8)]),
            remote("ah", src_hi, mid.at[:, pl.ds(0, 8)]),
            remote("pl", src_own, right.at[:, own]),
            remote("ph", src_own, left.at[:, own]),
            remote("alpl", src_lo, right.at[:, pl.ds(8 + nx, 8)]),
            remote("alph", src_lo, left.at[:, pl.ds(8 + nx, 8)]),
            remote("ahpl", src_hi, right.at[:, pl.ds(0, 8)]),
            remote("ahph", src_hi, left.at[:, pl.ds(0, 8)]),
        ]

    def layer_send(src_ref, src_index, y_at, side, slot, dst):
        return remote(
            side,
            src_ref.at[pl.ds(src_index, 1), pl.ds(y_at, ny)],
            dst.at[pl.ds(slot, 1), pl.ds(PAD, ny)],
        )

    plates_1 = plate_sends(u1.at[:, own], u1.at[:, pl.ds(8, 8)], u1.at[:, pl.ds(nx, 8)], u1, u1l, u1r)
    for number in plates_1:
        start(number)
    near_1 = [
        layer_send(p1, 2, PAD, "al", nx + 2, p1),
        layer_send(p1, nx + 1, PAD, "ah", 1, p1),
    ]
    far_1 = [
        layer_send(p1, 3, PAD, "al", nx + 3, p1),
        layer_send(p1, nx, PAD, "ah", 0, p1),
    ]
    cols_1 = [
        remote("pl", p1.at[pl.ds(2, nx), pl.ds(PAD, 8)], p1.at[pl.ds(2, nx), pl.ds(PAD + ny, 8)]),
        remote("ph", p1.at[pl.ds(2, nx), pl.ds(ny, 8)], p1.at[pl.ds(2, nx), pl.ds(0, 8)]),
    ]
    for number in near_1 + cols_1 + far_1:
        start(number)

    def prepare(value, x, sel):
        pieces = split_cat(value, 1)
        mx[x] = jnp.dot(pieces, band[...], preferred_element_type=F32)
        chosen = lax.dot_general(
            pick[...], pieces, (((1,), (1,)), ((), ())), preferred_element_type=F32
        )
        sel[pl.ds(x * 8, 8), :] = chosen[:8]

    def base(now, back, back_at, x, y0, count):
        at = PAD + y0
        nearest = (now[x + 1, pl.ds(at, count), :] + now[x + 3, pl.ds(at, count), :]) + (
            now[x + 2, pl.ds(at - 1, count), :] + now[x + 2, pl.ds(at + 1, count), :]
        )
        farther = (now[x, pl.ds(at, count), :] + now[x + 4, pl.ds(at, count), :]) + (
            now[x + 2, pl.ds(at - 2, count), :] + now[x + 2, pl.ds(at + 2, count), :]
        )
        held = back[x + back_at[0], pl.ds(y0 + back_at[1], count), :]
        return ((16.0 * nearest - farther) + mx[x, pl.ds(y0, count), :]) * (1.0 / 60.0) - held

    def pushed(x):
        return lax.dot_general(
            split_cat(drive[pl.ds(x * 8, 8), :], 0), weights[...],
            (((0,), (0,)), ((), ())), preferred_element_type=F32,
        ) * (1.0 / 60.0)

    mid_rows = ny - 16

    row_at = lax.broadcasted_iota(jnp.int32, (nx + 16, ny), 0) + (air * nx - 8)
    lane_at = lax.broadcasted_iota(jnp.int32, (nx + 16, ny), 1)
    col_at = lane_at + plate * ny

    def plate_update(mid, left, right, back_of, sel, sel_in, k):
        inside_rows = jnp.logical_and(row_at >= rows[0, k], row_at < rows[1, k])

        def masked(value, shift):
            c = col_at + shift
            inside = jnp.logical_and(c >= cols[0, k], c < cols[1, k])
            return jnp.where(jnp.logical_and(inside_rows, inside), value, 0.0)

        c = masked(mid[k], 0)
        lft = masked(left[k], -ny)
        rgt = masked(right[k], ny)
        ym1 = pltpu.roll(jnp.where(lane_at >= ny - 1, lft, c), 1, 1)
        ym2 = pltpu.roll(jnp.where(lane_at >= ny - 2, lft, c), 2, 1)
        yp1 = pltpu.roll(jnp.where(lane_at < 1, rgt, c), ny - 1, 1)
        yp2 = pltpu.roll(jnp.where(lane_at < 2, rgt, c), ny - 2, 1)
        around = ym1 + yp1
        beside = 2.0 * around - 8.0 * c
        total = nx + 16
        bih = (
            (20.0 * c - 8.0 * around + (ym2 + yp2))
            + (pltpu.roll(beside, 1, 0) + pltpu.roll(beside, total - 1, 0))
            + (pltpu.roll(c, 2, 0) + pltpu.roll(c, total - 2, 0))
        )[8 : 8 + nx]
        centre = c[8 : 8 + nx]
        mask = masked(jnp.ones((nx + 16, ny), F32), 0)[8 : 8 + nx]
        jump = sel[pl.ds(k, nx, stride=8), :] + sel_in[pl.ds(k, nx, stride=8), :]
        after = mask * (2.0 * centre - back_of(k, mask) - plate_step * bih - plate_load * jump)
        drive[pl.ds(k, nx, stride=8), :] = after - centre
        return after

    def take_edges(sel_in):
        for j in range(2):
            drive[pl.ds(plates + j, nx, stride=8), :] = sel_in[pl.ds(plates + j, nx, stride=8), :]

    for x in range(nx):
        prepare(p1[x + 2, pl.ds(PAD, ny), :], x, sel_1)
    swap_1 = remote("f", sel_1, sel_1_in)
    start(swap_1)
    loads[1].wait()
    loads[3].wait()
    first = (p1, p0, (0, 0))
    for x in range(2, nx - 2):
        p2[x + 2, pl.ds(PAD + 8, mid_rows), :] = base(*first, x, 8, mid_rows)
    for number in plates_1:
        arrive(number)
    arrive(swap_1)
    for k in range(plates):
        u2[k, own, :] = plate_update(
            u1, u1l, u1r, lambda k, mask: mask * u0[k], sel_1, sel_1_in, k
        )
    take_edges(sel_1_in)
    plates_2 = plate_sends(u2.at[:, own], u2.at[:, pl.ds(8, 8)], u2.at[:, pl.ds(nx, 8)], u2, u2l, u2r)
    for number in plates_2:
        start(number)
    for number in cols_1:
        arrive(number)

    def whole(x):
        p2[x + 2, pl.ds(PAD, ny), :] = base(*first, x, 0, ny) + pushed(x)

    arrive(near_1[1])
    whole(1)
    far_low = layer_send(p2, 3, PAD, "al", nx + 3, p2)
    start(far_low)
    arrive(near_1[0])
    whole(nx - 2)
    far_high = layer_send(p2, nx, PAD, "ah", 0, p2)
    start(far_high)
    arrive(far_1[1])
    whole(0)
    near_low = layer_send(p2, 2, PAD, "al", nx + 2, p2)
    start(near_low)
    arrive(far_1[0])
    whole(nx - 1)
    near_high = layer_send(p2, nx + 1, PAD, "ah", 1, p2)
    start(near_high)
    for x in range(2, nx - 2):
        more = pushed(x)
        p2[x + 2, pl.ds(PAD, 8), :] = base(*first, x, 0, 8) + more[:8]
        p2[x + 2, pl.ds(PAD + ny - 8, 8), :] = base(*first, x, ny - 8, 8) + more[ny - 8 :]
        p2[x + 2, pl.ds(PAD + 8, mid_rows), :] += more[8 : ny - 8]
    cols_2 = [
        remote("pl", p2.at[pl.ds(2, nx), pl.ds(PAD, 8)], p2.at[pl.ds(2, nx), pl.ds(PAD + ny, 8)]),
        remote("ph", p2.at[pl.ds(2, nx), pl.ds(ny, 8)], p2.at[pl.ds(2, nx), pl.ds(0, 8)]),
    ]
    for number in cols_2:
        start(number)
    for x in range(nx):
        prepare(p2[x + 2, pl.ds(PAD, ny), :], x, sel_2)
    swap_2 = remote("f", sel_2, sel_2_in)
    start(swap_2)
    stores = [
        pltpu.make_async_copy(p2.at[pl.ds(2, nx), pl.ds(PAD, ny)], out_before, local_sem.at[0]),
        pltpu.make_async_copy(u2.at[:, own], out_plate_before, local_sem.at[1]),
    ]
    for copy in stores:
        copy.start()

    second = (p2, p1, (2, PAD))
    for x in range(2, nx - 2):
        out_after[x, pl.ds(8, mid_rows), :] = base(*second, x, 8, mid_rows)
    for number in plates_2:
        arrive(number)
    arrive(swap_2)
    for k in range(plates):
        out_plate_after[k] = plate_update(
            u2, u2l, u2r, lambda k, mask: mask * u1[k, own, :], sel_2, sel_2_in, k
        )
    take_edges(sel_2_in)
    for x in range(nx):
        more = pushed(x)
        if 2 <= x < nx - 2:
            out_after[x, pl.ds(0, 8), :] = more[:8]
            out_after[x, pl.ds(ny - 8, 8), :] = more[ny - 8 :]
            out_after[x, pl.ds(8, mid_rows), :] += more[8 : ny - 8]
        else:
            out_after[x] = more
    for number in cols_2:
        arrive(number)
    for x in range(2, nx - 2):
        out_after[x, pl.ds(0, 8), :] += base(*second, x, 0, 8)
        out_after[x, pl.ds(ny - 8, 8), :] += base(*second, x, ny - 8, 8)
    arrive(far_high)
    arrive(near_high)
    for x in (0, 1):
        out_after[x] += base(*second, x, 0, ny)
    arrive(far_low)
    arrive(near_low)
    for x in (nx - 2, nx - 1):
        out_after[x] += base(*second, x, 0, ny)
    for number in range(len(made)):
        sent(number)
    for copy in stores:
        copy.wait()


REMOTES = 30


def put_kernel(*refs):
    count = (len(refs) - 1) // 2
    copies = [
        pltpu.make_async_copy(refs[i], refs[count + i], refs[-1].at[i]) for i in range(count)
    ]
    for copy in copies:
        copy.start()
    for copy in copies:
        copy.wait()


def on_device(counts, *arrays):
    air_prev, _, plate_prev, _, _, _, _ = arrays
    nx, ny, nz = air_prev.shape
    plates = plate_prev.shape[0]
    padded = pltpu.VMEM((nx + 4, ny + 2 * PAD, nz), F32)
    block = pltpu.VMEM((nx, ny, nz), F32)
    flat = pltpu.VMEM((nx * 8, ny), F32)
    tall = pltpu.VMEM((plates, nx + 16, ny), F32)
    tile = pltpu.VMEM((plates, nx, ny), F32)
    anywhere = pl.BlockSpec(memory_space=pl.ANY)
    stored = pl.BlockSpec(memory_space=pltpu.HBM)
    air = jax.ShapeDtypeStruct(air_prev.shape, F32)
    plate = jax.ShapeDtypeStruct(plate_prev.shape, F32)
    held_air = pltpu.VMEM(air.shape, F32)
    held_plate = pltpu.VMEM(plate.shape, F32)
    results = pl.pallas_call(
        functools.partial(kernel, counts),
        out_shape=(held_air, held_air, held_plate, held_plate),
        in_specs=[stored] * 7,
        out_specs=(pl.BlockSpec(memory_space=pltpu.VMEM),) * 4,
        scratch_shapes=[
            block, padded, padded, block, flat, flat, flat, flat, flat,
            tile, tall, tall, tall, tall, tall, tall,
            pltpu.VMEM((2 * nz, nz), BF16),
            pltpu.VMEM((16, 2 * nz), BF16),
            pltpu.VMEM((16, nz), BF16),
            pltpu.SMEM((plates,), jnp.int32),
            pltpu.SMEM((2, plates), jnp.int32),
            pltpu.SMEM((2, plates), jnp.int32),
            pltpu.SemaphoreType.DMA((7,)),
            pltpu.SemaphoreType.DMA((REMOTES,)),
            pltpu.SemaphoreType.DMA((REMOTES,)),
        ],
        compiler_params=pltpu.CompilerParams(
            collective_id=0, has_side_effects=True, vmem_limit_bytes=60 * 1024 * 1024
        ),
        cost_estimate=pl.CostEstimate(
            flops=50 * nx * ny * nz, bytes_accessed=16 * nx * ny * nz, transcendentals=0
        ),
    )(*arrays[:5], arrays[5].T, arrays[6].T)
    return pl.pallas_call(
        put_kernel,
        out_shape=(air, air, plate, plate),
        in_specs=[pl.BlockSpec(memory_space=pltpu.VMEM)] * 4,
        out_specs=(stored,) * 4,
        scratch_shapes=[pltpu.SemaphoreType.DMA((4,))],
        cost_estimate=pl.CostEstimate(
            flops=0, bytes_accessed=16 * nx * ny * nz, transcendentals=0
        ),
    )(*[pltpu.with_memory_space_constraint(one, pltpu.VMEM) for one in results])


def solution(mesh):
    counts = (mesh.shape["air"], mesh.shape["plate"])
    air = P(("groups", "air"), "plate", "field")
    plate = P("groups", "air", "plate")
    return jax.shard_map(
        functools.partial(on_device, counts),
        mesh=mesh,
        in_specs=(air, air, plate, plate, P("groups"), P("groups", None), P("groups", None)),
        out_specs=(air, air, plate, plate),
        check_vma=False,
    )
```

```python
import functools

import jax
import jax.numpy as jnp
from jax import lax
from jax.experimental import pallas as pl
from jax.experimental.pallas import tpu as pltpu
from jax.sharding import PartitionSpec as P

F32 = jnp.float32
BF16 = jnp.bfloat16
MESH = pl.DeviceIdType.MESH
plate_step = 0.05
plate_load = 0.3
PAD = 8


def split_cat(value, axis):
    high = value.astype(BF16)
    low = (value - high.astype(F32)).astype(BF16)
    if axis == 0:
        return jnp.concatenate([high.astype(F32), low.astype(F32)], axis=0).astype(BF16)
    return jnp.concatenate([high, low], axis=1)


def kernel(
    counts,
    air_prev, air_now, plate_prev, plate_now, height_in, rows_in, cols_in,
    out_after, out_before, out_plate_after, out_plate_before,
    p0, p1, p2, mx, sel_1, sel_1_in, sel_2, sel_2_in, drive,
    u0, u1, u1l, u1r, u2, u2l, u2r,
    band, pick, weights, height, rows, cols,
    local_sem, send_sem, recv_sem,
):
    n_air, n_plate = counts
    nx, ny, nz = p0.shape
    plates = u0.shape[0]
    air, plate, field = lax.axis_index("air"), lax.axis_index("plate"), lax.axis_index("field")
    has = {
        "al": air > 0, "ah": air < n_air - 1,
        "pl": plate > 0, "ph": plate < n_plate - 1,
    }
    for a in ("al", "ah"):
        for b in ("pl", "ph"):
            has[a + b] = jnp.logical_and(has[a], has[b])
    has["f"] = None
    where = {
        "al": {"air": air - 1}, "ah": {"air": air + 1},
        "pl": {"plate": plate - 1}, "ph": {"plate": plate + 1},
        "alpl": {"air": air - 1, "plate": plate - 1}, "alph": {"air": air - 1, "plate": plate + 1},
        "ahpl": {"air": air + 1, "plate": plate - 1}, "ahph": {"air": air + 1, "plate": plate + 1},
        "f": {"field": 1 - field},
    }
    swap = {"al": "ah", "ah": "al", "pl": "ph", "ph": "pl", "": "", "f": "f"}

    def opposite(side):
        return swap[side[:2]] + swap[side[2:]]

    def when(cond, fn):
        if cond is None:
            fn()
        else:
            pl.when(cond)(fn)

    made = []

    def remote(side, src, dst):
        number = len(made)
        copy = pltpu.make_async_remote_copy(
            src_ref=src, dst_ref=dst,
            send_sem=send_sem.at[number], recv_sem=recv_sem.at[number],
            device_id=where[side], device_id_type=MESH,
        )
        made.append((side, copy))
        return number

    def start(number):
        side, copy = made[number]
        when(has[side], lambda: copy.start())

    def arrive(number):
        side, copy = made[number]
        when(has[opposite(side)], lambda: copy.wait_recv())

    def sent(number):
        side, copy = made[number]
        when(has[side], lambda: copy.wait_send())

    loads = [
        pltpu.make_async_copy(
            air_now.at[pl.ds(2, nx - 4)], p1.at[pl.ds(4, nx - 4), pl.ds(PAD, ny)], local_sem.at[0]
        ),
        pltpu.make_async_copy(air_prev, p0, local_sem.at[1]),
        pltpu.make_async_copy(plate_now, u1.at[:, pl.ds(8, nx)], local_sem.at[2]),
        pltpu.make_async_copy(plate_prev, u0, local_sem.at[3]),
        pltpu.make_async_copy(height_in, height, local_sem.at[4]),
        pltpu.make_async_copy(rows_in, rows, local_sem.at[5]),
        pltpu.make_async_copy(cols_in, cols, local_sem.at[6]),
        pltpu.make_async_copy(
            air_now.at[pl.ds(0, 2)], p1.at[pl.ds(2, 2), pl.ds(PAD, ny)], local_sem.at[7]
        ),
        pltpu.make_async_copy(
            air_now.at[pl.ds(nx - 2, 2)], p1.at[pl.ds(nx, 2), pl.ds(PAD, ny)], local_sem.at[8]
        ),
    ]
    for copy in [loads[i] for i in (2, 7, 8, 4, 5, 6, 0, 1, 3)]:
        copy.start()

    barrier = pltpu.get_barrier_semaphore()
    total = jnp.int32(0)
    for side, target in where.items():
        def hail(target=target):
            pl.semaphore_signal(barrier, inc=1, device_id=target, device_id_type=MESH)
        when(has[side], hail)
        total = total + (1 if has[side] is None else has[side].astype(jnp.int32))
    for copy in loads[4:7]:
        copy.wait()
    depth_start = field * nz
    lane8 = lax.broadcasted_iota(jnp.int32, (8, nz), 1)
    row8 = lax.broadcasted_iota(jnp.int32, (8, nz), 0)
    profile = jnp.zeros((8, nz), F32)
    for k in range(plates):
        at = lane8 + (depth_start - height[k])
        step = jnp.where(at == 1, 1.0, 0.0) - jnp.where(at == -1, 1.0, 0.0)
        profile = jnp.where(row8 == k, step, profile)
    low_field = field == 0
    edge = jnp.where(low_field, nz - 2, 0) + (row8 - plates)
    is_edge = jnp.logical_and(row8 >= plates, row8 < plates + 2)
    picks = jnp.where(jnp.logical_and(is_edge, lane8 == edge), 1.0, profile)
    picks = jnp.concatenate([picks, jnp.zeros((8, nz), F32)], axis=0).astype(BF16)
    pick[...] = jnp.concatenate([picks, picks], axis=1)
    halo_lane = jnp.where(low_field, nz, -2) + (row8 - plates)
    gap = jnp.abs(lane8 - halo_lane)
    halo_weight = jnp.where(gap == 1, 16.0, jnp.where(gap == 2, -1.0, 0.0))
    wts = jnp.where(is_edge, halo_weight, 6.0 * profile)
    weights[...] = jnp.concatenate([wts, wts], axis=0).astype(BF16)
    gap = jnp.abs(
        lax.broadcasted_iota(jnp.int32, (nz, nz), 0) - lax.broadcasted_iota(jnp.int32, (nz, nz), 1)
    )
    one = jnp.where(
        gap == 0, 30.0, jnp.where(gap == 1, 16.0, jnp.where(gap == 2, -1.0, 0.0))
    ).astype(BF16)
    band[pl.ds(0, nz), :] = one
    band[pl.ds(nz, nz), :] = one
    drive[...] = jnp.zeros(drive.shape, F32)

    def clear(ref):
        def rows_low():
            ref[pl.ds(0, 2), pl.ds(PAD, ny), :] = jnp.zeros((2, ny, nz), F32)
        def rows_high():
            ref[pl.ds(nx + 2, 2), pl.ds(PAD, ny), :] = jnp.zeros((2, ny, nz), F32)
        def cols_low():
            ref[pl.ds(2, nx), pl.ds(0, 8), :] = jnp.zeros((nx, 8, nz), F32)
        def cols_high():
            ref[pl.ds(2, nx), pl.ds(PAD + ny, 8), :] = jnp.zeros((nx, 8, nz), F32)
        pl.when(jnp.logical_not(has["al"]))(rows_low)
        pl.when(jnp.logical_not(has["ah"]))(rows_high)
        pl.when(jnp.logical_not(has["pl"]))(cols_low)
        pl.when(jnp.logical_not(has["ph"]))(cols_high)

    clear(p1)
    clear(p2)

    for copy in (loads[2], loads[7], loads[8]):
        copy.wait()
    pl.semaphore_wait(barrier, total)

    own = pl.ds(8, nx)

    def plate_sends(src_own, src_lo, src_hi, mid, left, right):
        return [
            remote("al", src_lo, mid.at[:, pl.ds(8 + nx, 8)]),
            remote("ah", src_hi, mid.at[:, pl.ds(0, 8)]),
            remote("pl", src_own, right.at[:, own]),
            remote("ph", src_own, left.at[:, own]),
            remote("alpl", src_lo, right.at[:, pl.ds(8 + nx, 8)]),
            remote("alph", src_lo, left.at[:, pl.ds(8 + nx, 8)]),
            remote("ahpl", src_hi, right.at[:, pl.ds(0, 8)]),
            remote("ahph", src_hi, left.at[:, pl.ds(0, 8)]),
        ]

    def layer_send(src_ref, src_index, y_at, side, slot, dst):
        return remote(
            side,
            src_ref.at[pl.ds(src_index, 1), pl.ds(y_at, ny)],
            dst.at[pl.ds(slot, 1), pl.ds(PAD, ny)],
        )

    plates_1 = plate_sends(u1.at[:, own], u1.at[:, pl.ds(8, 8)], u1.at[:, pl.ds(nx, 8)], u1, u1l, u1r)
    for number in plates_1:
        start(number)
    near_1 = [
        layer_send(p1, 2, PAD, "al", nx + 2, p1),
        layer_send(p1, nx + 1, PAD, "ah", 1, p1),
    ]
    far_1 = [
        layer_send(p1, 3, PAD, "al", nx + 3, p1),
        layer_send(p1, nx, PAD, "ah", 0, p1),
    ]
    cols_1 = [
        remote("pl", p1.at[pl.ds(2, nx), pl.ds(PAD, 8)], p1.at[pl.ds(2, nx), pl.ds(PAD + ny, 8)]),
        remote("ph", p1.at[pl.ds(2, nx), pl.ds(ny, 8)], p1.at[pl.ds(2, nx), pl.ds(0, 8)]),
    ]
    for number in near_1 + far_1:
        start(number)
    loads[0].wait()
    for number in cols_1:
        start(number)

    def prepare(value, x, sel):
        pieces = split_cat(value, 1)
        mx[x] = jnp.dot(pieces, band[...], preferred_element_type=F32)
        chosen = lax.dot_general(
            pick[...], pieces, (((1,), (1,)), ((), ())), preferred_element_type=F32
        )
        sel[pl.ds(x * 8, 8), :] = chosen[:8]

    def base(now, back, back_at, x, y0, count):
        at = PAD + y0
        nearest = (now[x + 1, pl.ds(at, count), :] + now[x + 3, pl.ds(at, count), :]) + (
            now[x + 2, pl.ds(at - 1, count), :] + now[x + 2, pl.ds(at + 1, count), :]
        )
        farther = (now[x, pl.ds(at, count), :] + now[x + 4, pl.ds(at, count), :]) + (
            now[x + 2, pl.ds(at - 2, count), :] + now[x + 2, pl.ds(at + 2, count), :]
        )
        held = back[x + back_at[0], pl.ds(y0 + back_at[1], count), :]
        return ((16.0 * nearest - farther) + mx[x, pl.ds(y0, count), :]) * (1.0 / 60.0) - held

    def pushed(x):
        return lax.dot_general(
            split_cat(drive[pl.ds(x * 8, 8), :], 0), weights[...],
            (((0,), (0,)), ((), ())), preferred_element_type=F32,
        ) * (1.0 / 60.0)

    mid_rows = ny - 16

    row_at = lax.broadcasted_iota(jnp.int32, (nx + 16, ny), 0) + (air * nx - 8)
    lane_at = lax.broadcasted_iota(jnp.int32, (nx + 16, ny), 1)
    col_at = lane_at + plate * ny

    def plate_update(mid, left, right, back_of, sel, sel_in, k):
        inside_rows = jnp.logical_and(row_at >= rows[0, k], row_at < rows[1, k])

        def masked(value, shift):
            c = col_at + shift
            inside = jnp.logical_and(c >= cols[0, k], c < cols[1, k])
            return jnp.where(jnp.logical_and(inside_rows, inside), value, 0.0)

        c = masked(mid[k], 0)
        lft = masked(left[k], -ny)
        rgt = masked(right[k], ny)
        ym1 = pltpu.roll(jnp.where(lane_at >= ny - 1, lft, c), 1, 1)
        ym2 = pltpu.roll(jnp.where(lane_at >= ny - 2, lft, c), 2, 1)
        yp1 = pltpu.roll(jnp.where(lane_at < 1, rgt, c), ny - 1, 1)
        yp2 = pltpu.roll(jnp.where(lane_at < 2, rgt, c), ny - 2, 1)
        around = ym1 + yp1
        beside = 2.0 * around - 8.0 * c
        total = nx + 16
        bih = (
            (20.0 * c - 8.0 * around + (ym2 + yp2))
            + (pltpu.roll(beside, 1, 0) + pltpu.roll(beside, total - 1, 0))
            + (pltpu.roll(c, 2, 0) + pltpu.roll(c, total - 2, 0))
        )[8 : 8 + nx]
        centre = c[8 : 8 + nx]
        mask = masked(jnp.ones((nx + 16, ny), F32), 0)[8 : 8 + nx]
        jump = sel[pl.ds(k, nx, stride=8), :] + sel_in[pl.ds(k, nx, stride=8), :]
        after = mask * (2.0 * centre - back_of(k, mask) - plate_step * bih - plate_load * jump)
        drive[pl.ds(k, nx, stride=8), :] = after - centre
        return after

    def take_edges(sel_in):
        for j in range(2):
            drive[pl.ds(plates + j, nx, stride=8), :] = sel_in[pl.ds(plates + j, nx, stride=8), :]

    for x in range(nx):
        prepare(p1[x + 2, pl.ds(PAD, ny), :], x, sel_1)
    swap_1 = remote("f", sel_1, sel_1_in)
    start(swap_1)
    loads[1].wait()
    loads[3].wait()
    first = (p1, p0, (0, 0))
    for x in range(2, nx - 2):
        p2[x + 2, pl.ds(PAD + 8, mid_rows), :] = base(*first, x, 8, mid_rows)
    for number in plates_1:
        arrive(number)
    arrive(swap_1)
    for k in range(plates):
        u2[k, own, :] = plate_update(
            u1, u1l, u1r, lambda k, mask: mask * u0[k], sel_1, sel_1_in, k
        )
    take_edges(sel_1_in)
    plates_2 = plate_sends(u2.at[:, own], u2.at[:, pl.ds(8, 8)], u2.at[:, pl.ds(nx, 8)], u2, u2l, u2r)
    for number in plates_2:
        start(number)
    for number in cols_1:
        arrive(number)

    def whole(x):
        p2[x + 2, pl.ds(PAD, ny), :] = base(*first, x, 0, ny) + pushed(x)

    arrive(near_1[1])
    whole(1)
    far_low = layer_send(p2, 3, PAD, "al", nx + 3, p2)
    start(far_low)
    arrive(near_1[0])
    whole(nx - 2)
    far_high = layer_send(p2, nx, PAD, "ah", 0, p2)
    start(far_high)
    arrive(far_1[1])
    whole(0)
    near_low = layer_send(p2, 2, PAD, "al", nx + 2, p2)
    start(near_low)
    arrive(far_1[0])
    whole(nx - 1)
    near_high = layer_send(p2, nx + 1, PAD, "ah", 1, p2)
    start(near_high)
    for x in range(2, nx - 2):
        more = pushed(x)
        p2[x + 2, pl.ds(PAD, 8), :] = base(*first, x, 0, 8) + more[:8]
        p2[x + 2, pl.ds(PAD + ny - 8, 8), :] = base(*first, x, ny - 8, 8) + more[ny - 8 :]
        p2[x + 2, pl.ds(PAD + 8, mid_rows), :] += more[8 : ny - 8]
    cols_2 = [
        remote("pl", p2.at[pl.ds(2, nx), pl.ds(PAD, 8)], p2.at[pl.ds(2, nx), pl.ds(PAD + ny, 8)]),
        remote("ph", p2.at[pl.ds(2, nx), pl.ds(ny, 8)], p2.at[pl.ds(2, nx), pl.ds(0, 8)]),
    ]
    for number in cols_2:
        start(number)
    for x in range(nx):
        prepare(p2[x + 2, pl.ds(PAD, ny), :], x, sel_2)
    swap_2 = remote("f", sel_2, sel_2_in)
    start(swap_2)
    stores = [
        pltpu.make_async_copy(p2.at[pl.ds(2, nx), pl.ds(PAD, ny)], out_before, local_sem.at[0]),
        pltpu.make_async_copy(u2.at[:, own], out_plate_before, local_sem.at[1]),
    ]
    for copy in stores:
        copy.start()

    second = (p2, p1, (2, PAD))
    for x in range(2, nx - 2):
        out_after[x, pl.ds(8, mid_rows), :] = base(*second, x, 8, mid_rows)
    for number in plates_2:
        arrive(number)
    arrive(swap_2)
    for k in range(plates):
        out_plate_after[k] = plate_update(
            u2, u2l, u2r, lambda k, mask: mask * u1[k, own, :], sel_2, sel_2_in, k
        )
    take_edges(sel_2_in)
    for x in range(nx):
        more = pushed(x)
        if 2 <= x < nx - 2:
            out_after[x, pl.ds(0, 8), :] = more[:8]
            out_after[x, pl.ds(ny - 8, 8), :] = more[ny - 8 :]
            out_after[x, pl.ds(8, mid_rows), :] += more[8 : ny - 8]
        else:
            out_after[x] = more
    for number in cols_2:
        arrive(number)
    for x in range(2, nx - 2):
        out_after[x, pl.ds(0, 8), :] += base(*second, x, 0, 8)
        out_after[x, pl.ds(ny - 8, 8), :] += base(*second, x, ny - 8, 8)
    arrive(far_high)
    arrive(near_high)
    for x in (0, 1):
        out_after[x] += base(*second, x, 0, ny)
    arrive(far_low)
    arrive(near_low)
    for x in (nx - 2, nx - 1):
        out_after[x] += base(*second, x, 0, ny)
    for number in range(len(made)):
        sent(number)
    for copy in stores:
        copy.wait()


REMOTES = 30


def put_kernel(*refs):
    count = (len(refs) - 1) // 2
    copies = []
    for i in range(count):
        size = refs[i].shape[0]
        parts = 4 if size % 4 == 0 else 1
        for j in range(parts):
            piece = pl.ds(j * (size // parts), size // parts)
            copies.append(
                pltpu.make_async_copy(
                    refs[i].at[piece], refs[count + i].at[piece], refs[-1].at[len(copies)]
                )
            )
    for copy in copies:
        copy.start()
    for copy in copies:
        copy.wait()


def on_device(counts, *arrays):
    air_prev, _, plate_prev, _, _, _, _ = arrays
    nx, ny, nz = air_prev.shape
    plates = plate_prev.shape[0]
    padded = pltpu.VMEM((nx + 4, ny + 2 * PAD, nz), F32)
    block = pltpu.VMEM((nx, ny, nz), F32)
    flat = pltpu.VMEM((nx * 8, ny), F32)
    tall = pltpu.VMEM((plates, nx + 16, ny), F32)
    tile = pltpu.VMEM((plates, nx, ny), F32)
    anywhere = pl.BlockSpec(memory_space=pl.ANY)
    stored = pl.BlockSpec(memory_space=pltpu.HBM)
    air = jax.ShapeDtypeStruct(air_prev.shape, F32)
    plate = jax.ShapeDtypeStruct(plate_prev.shape, F32)
    held_air = pltpu.VMEM(air.shape, F32)
    held_plate = pltpu.VMEM(plate.shape, F32)
    results = pl.pallas_call(
        functools.partial(kernel, counts),
        out_shape=(held_air, held_air, held_plate, held_plate),
        in_specs=[stored] * 7,
        out_specs=(pl.BlockSpec(memory_space=pltpu.VMEM),) * 4,
        scratch_shapes=[
            block, padded, padded, block, flat, flat, flat, flat, flat,
            tile, tall, tall, tall, tall, tall, tall,
            pltpu.VMEM((2 * nz, nz), BF16),
            pltpu.VMEM((16, 2 * nz), BF16),
            pltpu.VMEM((16, nz), BF16),
            pltpu.SMEM((plates,), jnp.int32),
            pltpu.SMEM((2, plates), jnp.int32),
            pltpu.SMEM((2, plates), jnp.int32),
            pltpu.SemaphoreType.DMA((9,)),
            pltpu.SemaphoreType.DMA((REMOTES,)),
            pltpu.SemaphoreType.DMA((REMOTES,)),
        ],
        compiler_params=pltpu.CompilerParams(
            collective_id=0, has_side_effects=True, vmem_limit_bytes=60 * 1024 * 1024
        ),
        cost_estimate=pl.CostEstimate(
            flops=50 * nx * ny * nz, bytes_accessed=16 * nx * ny * nz, transcendentals=0
        ),
    )(*arrays[:5], arrays[5].T, arrays[6].T)
    return pl.pallas_call(
        put_kernel,
        out_shape=(air, air, plate, plate),
        in_specs=[pl.BlockSpec(memory_space=pltpu.VMEM)] * 4,
        out_specs=(stored,) * 4,
        scratch_shapes=[pltpu.SemaphoreType.DMA((16,))],
        cost_estimate=pl.CostEstimate(
            flops=0, bytes_accessed=16 * nx * ny * nz, transcendentals=0
        ),
    )(*[pltpu.with_memory_space_constraint(one, pltpu.VMEM) for one in results])


def solution(mesh):
    counts = (mesh.shape["air"], mesh.shape["plate"])
    air = P(("groups", "air"), "plate", "field")
    plate = P("groups", "air", "plate")
    return jax.shard_map(
        functools.partial(on_device, counts),
        mesh=mesh,
        in_specs=(air, air, plate, plate, P("groups"), P("groups", None), P("groups", None)),
        out_specs=(air, air, plate, plate),
        check_vma=False,
    )
```
